32 devices in a mesh: groups: 2 (over y), mp: 4 (over z), batch: 2 (over x), rep: 2 (over core).
Axes of the slice: x: 2, y: 2, z: 4, core: 2. Of those that a mesh axis runs over, the one named last changes fastest.
Arguments:
- attention_input: bfloat16 [1024, 8192], P(('groups', 'batch'), 'mp'), parts along dimension 0, may hold values from -6 to 6
- output_weight_matrix: bfloat16 [8192, 8192], P('mp', 'rep'), may hold values from -0.09375 to 0.09375
- down_factor_weights: bfloat16 [64, 8192, 64], P('batch', 'mp'), may hold values from -0.0625 to 0.0625
- up_factor_weights: bfloat16 [64, 64, 8192], P('batch', None, ('rep', 'mp')), may hold values from -0.75 to 0.75
- adapter_request_lists: int32 [4, 2, 4], P('groups'), parts along dimension 0, may hold values from 0 to 31, as said below
- request_adapter_slot: int32 [1024], P(('groups', 'batch')), parts along dimension 0, may hold values from 0 to 7, as said below
Outputs:
- projected: bfloat16 [1024, 8192], P(('groups', 'batch'), ('rep', 'mp')), parts along dimension 0
The draws below stay inside these ranges and needn't reach their ends.
There are 2 independent parts, one for each index of `groups`. The reference program is written for one: setup_inputs(seed, part) draws one part's arguments, and reference() takes and returns one part's arrays. A program takes and returns all parts, laid end to end along the dimension named above; an argument that names none is the same for every part. Nothing has to cross between parts.
Inputs may be any that keep to these rules, and one draw needn't show every extreme that they name: Each entry adapter_request_lists[b, h] holds 4 distinct numbers. `request_adapter_slot`: every slot appears among the requests of each index of batch.
All inputs are finite; a program needn't handle non-finite values.
Results may differ from the reference program's by a relative error of at most 0.0024.
Values may be sent and summed in bfloat16 or wider, within the bound.
A program may use at most 128 MiB of HBM per device.

```python
import jax
import jax.numpy as jnp
from jax import lax

MODEL_WIDTH = 8192
ADAPTER_RANK = 64
RQ_DEV = 256
ADP_DEV = 32
CAP = 4
NEED = 8
ADAPTER_TOTAL = 64
REQUESTS = 512
N_BATCH = 2


def draw_adapter_request_lists(key, part):
    key = jax.random.fold_in(key, 11)
    keys = jax.random.split(key, N_BATCH * N_BATCH)
    perms = jax.vmap(lambda k: jax.random.permutation(k, ADP_DEV))(keys)[:, :CAP].astype(jnp.int32)
    first = perms[:, 0]
    target = first.at[0].set(ADP_DEV - 1).at[1].set(0)
    offset = target - first
    rotated = (perms + offset[:, None]) % ADP_DEV
    return rotated.reshape(N_BATCH, N_BATCH, CAP).astype(jnp.int32)


def slot_block(key):
    keys = jax.random.split(key, 5)
    cover = jax.random.permutation(keys[0], NEED).astype(jnp.int32)
    popular = jax.random.permutation(keys[1], NEED).astype(jnp.int32)
    first_pick = jax.random.randint(keys[2], (RQ_DEV,), 0, NEED)
    second_pick = jax.random.randint(keys[3], (RQ_DEV,), 0, NEED)
    skewed = popular[jnp.minimum(first_pick, second_pick)]
    block = jnp.concatenate([cover, skewed[NEED:]])
    return block[jax.random.permutation(keys[4], RQ_DEV)].astype(jnp.int32)


def draw_request_adapter_slot(key, part):
    key = jax.random.fold_in(key, 23)
    keys = jax.random.split(key, N_BATCH)
    return jax.vmap(slot_block)(keys).reshape(REQUESTS).astype(jnp.int32)


def with_spikes(result, key, source, target, shards_of, factor):
    def block_of(axis_at):
        return (jnp.arange(result.shape[axis_at]) // (result.shape[axis_at] // shards_of)).reshape((-1,) + (1,) * (result.ndim - 1 - axis_at))

    one_side = jax.random.permutation(key, shards_of)[block_of(target)]
    other_side = (block_of(target) + shards_of // 2) % shards_of
    return jnp.where((block_of(source) == one_side) | (block_of(source) == other_side), factor * result, result)


def block_scale(rng, shape, cuts, low, high):
    gain, own = 1.0, jax.random.fold_in(rng, 6)
    for dim, shards_of in cuts:
        steps = jnp.exp(jax.random.uniform(jax.random.fold_in(own, dim), (shards_of,), jnp.float32, low / len(cuts), high / len(cuts)))
        gain = gain * jnp.repeat(steps, shape[dim] // shards_of).reshape([-1 if axis == dim else 1 for axis in range(len(shape))])
    return gain


def gaussian(own_key, dims, width, bound, pieces=(), kind=jnp.bfloat16):
    level = block_scale(own_key, dims, pieces, -0.22, 0.18) if pieces else 1.0
    values = jax.random.normal(own_key, dims, jnp.float32) * width * level
    return jnp.minimum(jnp.maximum(values, -bound), bound).astype(kind)


def noise_with(key, extent, deviation, bound, cuts, heavy, dtype=jnp.bfloat16):
    values = deviation * jax.random.normal(key, extent, jnp.float32)
    if cuts:
        values = values * block_scale(key, extent, cuts, -0.22, 0.18)
    return jnp.clip(with_spikes(values, jax.random.fold_in(key, 3), *heavy), -bound, bound).astype(dtype)


def setup_inputs(seed: int = 0, part: int = 0) -> dict:
    key_list = jax.random.split(jax.random.key(seed), 7)
    part_splits = jax.random.split(jax.random.fold_in(key_list[6], part), 7)
    attention_input = gaussian(part_splits[0], (REQUESTS, MODEL_WIDTH), 1.0, 6.0, ((0, 2), (1, 4)))
    output_weight_matrix = noise_with(key_list[1], (MODEL_WIDTH, MODEL_WIDTH), MODEL_WIDTH ** -0.5, 0.09375, ((0, 4), (1, 2)), (0, 1, 4, 2.0))
    down_factor_weights = gaussian(key_list[2], (ADAPTER_TOTAL, MODEL_WIDTH, ADAPTER_RANK), MODEL_WIDTH ** -0.5, 0.0625, ((0, 2), (1, 4)))
    up_factor_weights = gaussian(key_list[3], (ADAPTER_TOTAL, ADAPTER_RANK, MODEL_WIDTH), ADAPTER_RANK ** -0.5, 0.75, ((0, 2), (2, 8)))
    adapter_request_lists = draw_adapter_request_lists(jax.random.fold_in(jax.random.fold_in(key_list[6], part), 71), part)
    request_adapter_slot = draw_request_adapter_slot(jax.random.fold_in(jax.random.fold_in(key_list[6], part), 71), part)
    return {"attention_input": attention_input, "output_weight_matrix": output_weight_matrix, "down_factor_weights": down_factor_weights, "up_factor_weights": up_factor_weights, "adapter_request_lists": adapter_request_lists, "request_adapter_slot": request_adapter_slot}


def reference(attention_input, output_weight_matrix, down_factor_weights, up_factor_weights, adapter_request_lists, request_adapter_slot):
    base = jnp.dot(attention_input, output_weight_matrix, preferred_element_type=jnp.float32)
    batch_row = (jnp.arange(REQUESTS) // RQ_DEV).astype(jnp.int32)
    home = request_adapter_slot // CAP
    within = request_adapter_slot % CAP
    adapter = (home * ADP_DEV + adapter_request_lists[batch_row, home, within]).astype(jnp.int32)

    def one_shrink(paired_entry):
        return jnp.dot(paired_entry[0], down_factor_weights[paired_entry[1]], preferred_element_type=jnp.float32)

    shrink = lax.map(one_shrink, (attention_input, adapter)).astype(jnp.bfloat16)

    def one_expand(paired_entry):
        return jnp.dot(paired_entry[0], up_factor_weights[paired_entry[1]], preferred_element_type=jnp.float32)

    expand = lax.map(one_expand, (shrink, adapter))
    return (base + 0.5 * expand).astype(jnp.bfloat16)
```

```python
import functools

import jax
import jax.numpy as jnp
from jax import lax
from jax.experimental import pallas as pl
from jax.experimental.pallas import tpu as pltpu
from jax.sharding import PartitionSpec as P

MESH = pl.DeviceIdType.MESH
TOP = 32766.0
DEPTH = 2
AHEAD = 2


def kernel(
    n, reps, nb, cw,
    x_hbm, w_hbm, a_hbm, b_hbm, lists, slot_ref, out_ref,
    x_v, w_v, a_all, b_all, a_snd, a_tab, b_snd, b_tab,
    snd, snd_scale, rcv, rcv_scale, rs_snd, rs_rcv, ag, spread, acc,
    x_sem, w_sem, ab_sem, snd_sem, snd_scale_sem, rcv_sem, rcv_scale_sem,
    xs_sem, xr_sem, small_sem,
):
    me, rep, mine = lax.axis_index("mp"), lax.axis_index("rep"), lax.axis_index("batch")
    chunks = acc.shape[0]
    steps = (n - 1) * chunks
    cap = lists.shape[2]
    half = cap // reps
    rank = a_tab.shape[2]
    nd = n * reps
    lin = me * reps + rep
    counts = ((n - 1 - me) * chunks, me * chunks)

    def w_copy(q):
        return pltpu.make_async_copy(
            w_hbm.at[:, pl.ds(pl.multiple_of(q * cw, cw), cw)], w_v.at[q], w_sem.at[q]
        )

    def chunk_of(t, d):
        s, c = t // chunks, t % chunks
        return ((n - 1 - s) if d == 0 else s) * chunks + c

    def fetch(t):
        for d in range(2):
            @pl.when(t < counts[d])
            def _():
                w_copy(chunk_of(t, d)).start()

    x_copy = pltpu.make_async_copy(x_hbm, x_v, x_sem)
    a_copy = pltpu.make_async_copy(a_hbm, a_all, ab_sem.at[0])
    b_copy = pltpu.make_async_copy(b_hbm, b_all, ab_sem.at[1])
    x_copy.start()
    for t in range(AHEAD):
        fetch(t)
    a_copy.start()

    barrier = pltpu.get_barrier_semaphore()

    def peer(k):
        p = lax.rem(lin + k, nd)
        return p, {"mp": p // reps, "rep": lax.rem(p, reps)}

    for k in range(1, nb):
        pl.semaphore_signal(
            barrier, inc=1, device_id={"batch": lax.rem(mine + k, nb)}, device_id_type=MESH
        )

    def greet(k, carry):
        pl.semaphore_signal(barrier, inc=1, device_id=peer(k)[1], device_id_type=MESH)
        return carry

    lax.fori_loop(1, nd, greet, 0)
    pl.semaphore_wait(barrier, nd - 1 + nb - 1)
    x_copy.wait()

    def sends(t, d):
        to = {"mp": me + 1 if d == 0 else me - 1}
        return (
            pltpu.make_async_remote_copy(
                snd.at[d, t % DEPTH], rcv.at[d, t], snd_sem.at[d, t % DEPTH],
                rcv_sem.at[d, t], device_id=to, device_id_type=MESH,
            ),
            pltpu.make_async_remote_copy(
                snd_scale.at[d, t % DEPTH], rcv_scale.at[d, t], snd_scale_sem.at[d, t % DEPTH],
                rcv_scale_sem.at[d, t], device_id=to, device_id_type=MESH,
            ),
        )

    def a_send(k):
        return pltpu.make_async_remote_copy(
            a_snd.at[k - 1], a_tab.at[mine], xs_sem.at[0, k - 1], xr_sem.at[0, k - 1],
            device_id={"batch": lax.rem(mine + k, nb)}, device_id_type=MESH,
        )

    def b_send(k):
        return pltpu.make_async_remote_copy(
            b_snd.at[k - 1], b_tab.at[mine], xs_sem.at[1, k - 1], xr_sem.at[1, k - 1],
            device_id={"batch": lax.rem(mine + k, nb)}, device_id_type=MESH,
        )

    def rs_send(k):
        p, to = peer(k)
        return pltpu.make_async_remote_copy(
            rs_snd.at[p], rs_rcv.at[k - 1], small_sem.at[0], small_sem.at[1],
            device_id=to, device_id_type=MESH,
        )

    def ag_send(k):
        return pltpu.make_async_remote_copy(
            ag.at[lin], ag.at[lin], small_sem.at[2], small_sem.at[3],
            device_id=peer(k)[1], device_id_type=MESH,
        )

    def all_small(buf, i):
        part = buf.at[pl.ds(0, nd - 1)]
        return pltpu.make_async_remote_copy(
            part, part, small_sem.at[i], small_sem.at[i + 1],
            device_id=peer(1)[1], device_id_type=MESH,
        )

    def pick_down():
        a_copy.wait()
        for k in range(1, nb):
            to = lax.rem(mine + k, nb)
            for j in range(half):
                a_snd[k - 1, j] = a_all[lists[to, mine, rep * half + j]]
            a_send(k).start()
        for j in range(half):
            a_tab[mine, j] = a_all[lists[mine, mine, rep * half + j]]

    def pick_up():
        b_copy.wait()
        for k in range(1, nb):
            to = lax.rem(mine + k, nb)
            for j in range(cap):
                b_snd[k - 1, j] = b_all[lists[to, mine, j]]
            b_send(k).start()
        for j in range(cap):
            b_tab[mine, j] = b_all[lists[mine, mine, j]]

    def shrink_part():
        for k in range(1, nb):
            a_send(k).wait()
        total = jnp.zeros((rank, x_v.shape[0]), jnp.float32)
        for h in range(nb):
            every = lax.dot_general(
                a_tab[h].reshape(half * rank, a_tab.shape[3]), x_v[...],
                (((1,), (1,)), ((), ())), preferred_element_type=jnp.float32,
            )
            for j in range(half):
                here = slot_ref[...] == h * cap + rep * half + j
                total += jnp.where(here, every[j * rank:(j + 1) * rank], 0.0)
        rr = rank // nd
        for p in range(nd):
            rs_snd[p] = total[p * rr:(p + 1) * rr]

        def go(k, carry):
            rs_send(k).start()
            return carry

        lax.fori_loop(1, nd, go, 0)

    def shrink_sum():
        all_small(rs_rcv, 0).wait()
        total = rs_snd[lin]
        for k in range(nd - 1):
            total += rs_rcv[k]
        ag[lin] = total.astype(jnp.bfloat16).astype(jnp.float32)

        def go(k, carry):
            ag_send(k).start()
            return carry

        lax.fori_loop(1, nd, go, 0)

    def decoded(d, t):
        for copy in sends(t, d):
            copy.wait_recv()
        return rcv[d, t].astype(jnp.int32).astype(jnp.float32) * rcv_scale[d, t]

    def step(t, carry):
        fetch(t + AHEAD)

        @pl.when(t < chunks)
        def _():
            w_copy(me * chunks + t).start()

        @pl.when(t == 0)
        def _():
            b_copy.start()

        for d in range(2):
            @pl.when(t < counts[d])
            def _():
                q = chunk_of(t, d)
                w_copy(q).wait()
                acc[0] = jnp.dot(x_v[...], w_v[q], preferred_element_type=jnp.float32)

                @pl.when(me > 0 if d == 0 else me < n - 1)
                def _():
                    acc[0] += decoded(d, t)

                @pl.when(t >= DEPTH)
                def _():
                    for copy in sends(t - DEPTH, d):
                        copy.wait_send()

                value = acc[0]
                most = jnp.maximum(jnp.max(jnp.abs(value), axis=0, keepdims=True), 1e-30)
                code = jnp.round(value * (TOP / most))
                snd[d, t % DEPTH] = code.astype(jnp.int32).astype(jnp.int16)
                snd_scale[d, t % DEPTH] = most * (1.0 / TOP)
                for copy in sends(t, d):
                    copy.start()

        for at, stage in ((1, pick_down), (2, pick_up), (steps // 2, shrink_part), (2 * steps // 3, shrink_sum)):
            pl.when(t == at)(stage)
        return carry

    lax.fori_loop(0, steps, step, 0)

    all_small(ag, 2).wait()
    low = ag[...].reshape(rank, x_v.shape[0])
    for s in range(nb * cap):
        here = slot_ref[...] == s
        spread[s * rank:(s + 1) * rank] = jnp.where(here, low, 0.0).astype(jnp.bfloat16)
    for k in range(1, nb):
        b_send(k).wait()
    for c in range(chunks):
        w_copy(me * chunks + c).wait()
        table = b_tab[:, :, :, c * cw:(c + 1) * cw].reshape(nb * cap * rank, cw)
        acc[c] = jnp.dot(
            x_v[...], w_v[me * chunks + c], preferred_element_type=jnp.float32
        ) + 0.5 * lax.dot_general(
            spread[...], table, (((0,), (0,)), ((), ())), preferred_element_type=jnp.float32
        )
    for c in range(chunks):
        for d in range(2):
            @pl.when(me > 0 if d == 0 else me < n - 1)
            def _():
                acc[c] += decoded(d, counts[d] + c)
        out_ref[:, c * cw:(c + 1) * cw] = acc[c].astype(out_ref.dtype)

    for d in range(2):
        def drain(t, carry):
            for copy in sends(t, d):
                copy.wait_send()
            return carry

        lax.fori_loop(jnp.maximum(counts[d] - DEPTH, 0), counts[d], drain, 0)


def solution(mesh):
    n, reps, nb = mesh.shape["mp"], mesh.shape["rep"], mesh.shape["batch"]

    def per_device(x, w, down, up, lists, slots):
        rows, depth = x.shape
        adapters, _, rank = down.shape
        width = up.shape[2]
        cap = lists.shape[2]
        half = cap // reps
        cw = min(256, width)
        chunks = width // cw
        steps = (n - 1) * chunks
        nd = n * reps
        bf, f32 = jnp.bfloat16, jnp.float32
        dma = pltpu.SemaphoreType.DMA
        hbm = pl.BlockSpec(memory_space=pl.ANY)
        vmem = pl.BlockSpec(memory_space=pltpu.VMEM)
        return pl.pallas_call(
            functools.partial(kernel, n, reps, nb, cw),
            out_shape=jax.ShapeDtypeStruct((rows, width), bf),
            in_specs=[hbm] * 4 + [pl.BlockSpec(memory_space=pltpu.SMEM), vmem],
            out_specs=vmem,
            scratch_shapes=[
                pltpu.VMEM((rows, depth), bf),
                pltpu.VMEM((n * chunks, depth, cw), bf),
                pltpu.VMEM((adapters, rank, depth), bf),
                pltpu.VMEM((adapters, rank, width), bf),
                pltpu.VMEM((nb - 1, half, rank, depth), bf),
                pltpu.VMEM((nb, half, rank, depth), bf),
                pltpu.VMEM((nb - 1, cap, rank, width), bf),
                pltpu.VMEM((nb, cap, rank, width), bf),
                pltpu.VMEM((2, DEPTH, rows, cw), jnp.int16),
                pltpu.VMEM((2, DEPTH, 1, cw), f32),
                pltpu.VMEM((2, steps, rows, cw), jnp.int16),
                pltpu.VMEM((2, steps, 1, cw), f32),
                pltpu.VMEM((nd, rank // nd, rows), f32),
                pltpu.VMEM((nd, rank // nd, rows), f32),
                pltpu.VMEM((nd, rank // nd, rows), f32),
                pltpu.VMEM((nb * cap * rank, rows), bf),
                pltpu.VMEM((chunks, rows, cw), f32),
                dma,
                dma((n * chunks,)),
                dma((2,)),
                dma((2, DEPTH)),
                dma((2, DEPTH)),
                dma((2, steps)),
                dma((2, steps)),
                dma((2, nb - 1)),
                dma((2, nb - 1)),
                dma((4,)),
            ],
            compiler_params=pltpu.CompilerParams(
                collective_id=0, has_side_effects=True, vmem_limit_bytes=56 * 1024 * 1024
            ),
            cost_estimate=pl.CostEstimate(
                flops=2 * rows * depth * w.shape[1], bytes_accessed=2 * w.size, transcendentals=0
            ),
        )(x, w, jnp.swapaxes(down, 1, 2), up, lists, slots.reshape(1, rows))

    in_specs = (
        P(("groups", "batch"), "mp"),
        P("mp", "rep"),
        P("batch", "mp", None),
        P("batch", None, ("rep", "mp")),
        P("groups", None, None),
        P(("groups", "batch")),
    )
    out_specs = P(("groups", "batch"), ("rep", "mp"))
    return jax.shard_map(
        per_device, mesh=mesh, in_specs=in_specs, out_specs=out_specs, check_vma=False
    )
```

```python
import functools

import jax
import jax.numpy as jnp
from jax import lax
from jax.experimental import pallas as pl
from jax.experimental.pallas import tpu as pltpu
from jax.sharding import PartitionSpec as P

MESH = pl.DeviceIdType.MESH
TOP = 32766.0
DEPTH = 2
AHEAD = 2
LAG = 2
OWN = 0


def kernel(
    n, reps, nb, cw,
    x_hbm, w_hbm, a_hbm, b_hbm, lists, slot_ref, out_ref,
    x_v, w_v, a_all, b_all, a_snd, a_tab, b_snd, b_tab,
    snd, snd_scale, rcv, rcv_scale, rs_snd, rs_rcv, ag, spread, acc,
    x_sem, w_sem, ab_sem, snd_sem, snd_scale_sem, rcv_sem, rcv_scale_sem,
    xs_sem, xr_sem, small_sem,
):
    me, rep, mine = lax.axis_index("mp"), lax.axis_index("rep"), lax.axis_index("batch")
    chunks = acc.shape[0]
    steps = (n - 1) * chunks
    cap = lists.shape[2]
    half = cap // reps
    rank = a_tab.shape[2]
    nd = n * reps
    lin = me * reps + rep
    counts = ((n - 1 - me) * chunks, me * chunks)

    def w_copy(q):
        return pltpu.make_async_copy(
            w_hbm.at[:, pl.ds(pl.multiple_of(q * cw, cw), cw)], w_v.at[q], w_sem.at[q]
        )

    def chunk_of(t, d):
        s, c = t // chunks, t % chunks
        return ((n - 1 - s) if d == 0 else s) * chunks + c

    def fetch(tick):
        for d in range(2):
            t = tick - LAG * (me if d == 0 else n - 1 - me)

            @pl.when((t >= 0) & (t < counts[d]))
            def _():
                w_copy(chunk_of(t, d)).start()

    x_copy = pltpu.make_async_copy(x_hbm, x_v, x_sem)
    a_copy = pltpu.make_async_copy(a_hbm, a_all, ab_sem.at[0])
    b_copy = pltpu.make_async_copy(b_hbm, b_all, ab_sem.at[1])
    x_copy.start()
    for t in range(AHEAD):
        fetch(t)
    a_copy.start()

    barrier = pltpu.get_barrier_semaphore()

    def peer(k):
        p = lax.rem(lin + k, nd)
        return p, {"mp": p // reps, "rep": lax.rem(p, reps)}

    for k in range(1, nb):
        pl.semaphore_signal(
            barrier, inc=1, device_id={"batch": lax.rem(mine + k, nb)}, device_id_type=MESH
        )

    def greet(k, carry):
        pl.semaphore_signal(barrier, inc=1, device_id=peer(k)[1], device_id_type=MESH)
        return carry

    lax.fori_loop(1, nd, greet, 0)
    pl.semaphore_wait(barrier, nd - 1 + nb - 1)
    x_copy.wait()

    def sends(t, d):
        to = {"mp": me + 1 if d == 0 else me - 1}
        return (
            pltpu.make_async_remote_copy(
                snd.at[d, t % DEPTH], rcv.at[d, t], snd_sem.at[d, t % DEPTH],
                rcv_sem.at[d, t], device_id=to, device_id_type=MESH,
            ),
            pltpu.make_async_remote_copy(
                snd_scale.at[d, t % DEPTH], rcv_scale.at[d, t], snd_scale_sem.at[d, t % DEPTH],
                rcv_scale_sem.at[d, t], device_id=to, device_id_type=MESH,
            ),
        )

    def a_send(k):
        return pltpu.make_async_remote_copy(
            a_snd.at[k - 1], a_tab.at[mine], xs_sem.at[0, k - 1], xr_sem.at[0, k - 1],
            device_id={"batch": lax.rem(mine + k, nb)}, device_id_type=MESH,
        )

    def b_send(k):
        return pltpu.make_async_remote_copy(
            b_snd.at[k - 1], b_tab.at[mine], xs_sem.at[1, k - 1], xr_sem.at[1, k - 1],
            device_id={"batch": lax.rem(mine + k, nb)}, device_id_type=MESH,
        )

    def rs_send(k):
        p, to = peer(k)
        return pltpu.make_async_remote_copy(
            rs_snd.at[p], rs_rcv.at[k - 1], small_sem.at[0], small_sem.at[1],
            device_id=to, device_id_type=MESH,
        )

    def ag_send(k):
        return pltpu.make_async_remote_copy(
            ag.at[lin], ag.at[lin], small_sem.at[2], small_sem.at[3],
            device_id=peer(k)[1], device_id_type=MESH,
        )

    def all_small(buf, i):
        part = buf.at[pl.ds(0, nd - 1)]
        return pltpu.make_async_remote_copy(
            part, part, small_sem.at[i], small_sem.at[i + 1],
            device_id=peer(1)[1], device_id_type=MESH,
        )

    def pick_down():
        a_copy.wait()
        for k in range(1, nb):
            to = lax.rem(mine + k, nb)
            for j in range(half):
                a_snd[k - 1, j] = a_all[lists[to, mine, rep * half + j]]
            a_send(k).start()
        for j in range(half):
            a_tab[mine, j] = a_all[lists[mine, mine, rep * half + j]]

    def pick_up():
        b_copy.wait()
        for k in range(1, nb):
            to = lax.rem(mine + k, nb)
            for j in range(cap):
                b_snd[k - 1, j] = b_all[lists[to, mine, j]]
            b_send(k).start()
        for j in range(cap):
            b_tab[mine, j] = b_all[lists[mine, mine, j]]

    def shrink_part():
        for k in range(1, nb):
            a_send(k).wait()
        total = jnp.zeros((rank, x_v.shape[0]), jnp.float32)
        for h in range(nb):
            every = lax.dot_general(
                a_tab[h].reshape(half * rank, a_tab.shape[3]), x_v[...],
                (((1,), (1,)), ((), ())), preferred_element_type=jnp.float32,
            )
            for j in range(half):
                here = slot_ref[...] == h * cap + rep * half + j
                total += jnp.where(here, every[j * rank:(j + 1) * rank], 0.0)
        rr = rank // nd
        for p in range(nd):
            rs_snd[p] = total[p * rr:(p + 1) * rr]

        def go(k, carry):
            rs_send(k).start()
            return carry

        lax.fori_loop(1, nd, go, 0)

    def shrink_sum():
        all_small(rs_rcv, 0).wait()
        total = rs_snd[lin]
        for k in range(nd - 1):
            total += rs_rcv[k]
        ag[lin] = total.astype(jnp.bfloat16).astype(jnp.float32)

        def go(k, carry):
            ag_send(k).start()
            return carry

        lax.fori_loop(1, nd, go, 0)

    def decoded(d, t):
        for copy in sends(t, d):
            copy.wait_recv()
        return rcv[d, t].astype(jnp.int32).astype(jnp.float32) * rcv_scale[d, t]

    hops = (me, n - 1 - me)

    def step(tick, carry):
        for d in range(2):
            t = tick - LAG * hops[d]

            @pl.when((t + AHEAD >= 0) & (t + AHEAD < counts[d]))
            def _():
                w_copy(chunk_of(t + AHEAD, d)).start()

            @pl.when((t >= 0) & (t < counts[d]))
            def _():
                q = chunk_of(t, d)
                w_copy(q).wait()
                acc[0] = jnp.dot(x_v[...], w_v[q], preferred_element_type=jnp.float32)

                @pl.when(hops[d] > 0)
                def _():
                    acc[0] += decoded(d, t)

                @pl.when(t >= DEPTH)
                def _():
                    for copy in sends(t - DEPTH, d):
                        copy.wait_send()

                value = acc[0]
                most = jnp.maximum(jnp.max(jnp.abs(value), axis=0, keepdims=True), 1e-30)
                code = jnp.round(value * (TOP / most))
                snd[d, t % DEPTH] = code.astype(jnp.int32).astype(jnp.int16)
                snd_scale[d, t % DEPTH] = most * (1.0 / TOP)
                for copy in sends(t, d):
                    copy.start()

        @pl.when(tick == 0)
        def _():
            b_copy.start()

        @pl.when((tick >= OWN) & (tick < OWN + chunks))
        def _():
            w_copy(me * chunks + tick - OWN).start()

        for at, stage in ((1, pick_down), (2, pick_up), (steps // 2, shrink_part), (2 * steps // 3, shrink_sum)):
            pl.when(tick == at)(stage)
        return carry

    lax.fori_loop(0, (n - 1) * max(chunks, LAG) + OWN, step, 0)

    all_small(ag, 2).wait()
    low = ag[...].reshape(rank, x_v.shape[0])
    for s in range(nb * cap):
        here = slot_ref[...] == s
        spread[s * rank:(s + 1) * rank] = jnp.where(here, low, 0.0).astype(jnp.bfloat16)
    for k in range(1, nb):
        b_send(k).wait()
    for c in range(chunks):
        w_copy(me * chunks + c).wait()
        table = b_tab[:, :, :, c * cw:(c + 1) * cw].reshape(nb * cap * rank, cw)
        acc[c] = jnp.dot(
            x_v[...], w_v[me * chunks + c], preferred_element_type=jnp.float32
        ) + 0.5 * lax.dot_general(
            spread[...], table, (((0,), (0,)), ((), ())), preferred_element_type=jnp.float32
        )
    for c in range(chunks):
        for d in range(2):
            @pl.when(me > 0 if d == 0 else me < n - 1)
            def _():
                acc[c] += decoded(d, counts[d] + c)
        out_ref[:, c * cw:(c + 1) * cw] = acc[c].astype(out_ref.dtype)

    for d in range(2):
        def drain(t, carry):
            for copy in sends(t, d):
                copy.wait_send()
            return carry

        lax.fori_loop(jnp.maximum(counts[d] - DEPTH, 0), counts[d], drain, 0)


def solution(mesh):
    n, reps, nb = mesh.shape["mp"], mesh.shape["rep"], mesh.shape["batch"]

    def per_device(x, w, down, up, lists, slots):
        rows, depth = x.shape
        adapters, _, rank = down.shape
        width = up.shape[2]
        cap = lists.shape[2]
        half = cap // reps
        cw = min(256, width)
        chunks = width // cw
        steps = (n - 1) * chunks
        nd = n * reps
        bf, f32 = jnp.bfloat16, jnp.float32
        dma = pltpu.SemaphoreType.DMA
        hbm = pl.BlockSpec(memory_space=pl.ANY)
        vmem = pl.BlockSpec(memory_space=pltpu.VMEM)
        return pl.pallas_call(
            functools.partial(kernel, n, reps, nb, cw),
            out_shape=jax.ShapeDtypeStruct((rows, width), bf),
            in_specs=[hbm] * 4 + [pl.BlockSpec(memory_space=pltpu.SMEM), vmem],
            out_specs=vmem,
            scratch_shapes=[
                pltpu.VMEM((rows, depth), bf),
                pltpu.VMEM((n * chunks, depth, cw), bf),
                pltpu.VMEM((adapters, rank, depth), bf),
                pltpu.VMEM((adapters, rank, width), bf),
                pltpu.VMEM((nb - 1, half, rank, depth), bf),
                pltpu.VMEM((nb, half, rank, depth), bf),
                pltpu.VMEM((nb - 1, cap, rank, width), bf),
                pltpu.VMEM((nb, cap, rank, width), bf),
                pltpu.VMEM((2, DEPTH, rows, cw), jnp.int16),
                pltpu.VMEM((2, DEPTH, 1, cw), f32),
                pltpu.VMEM((2, steps, rows, cw), jnp.int16),
                pltpu.VMEM((2, steps, 1, cw), f32),
                pltpu.VMEM((nd, rank // nd, rows), f32),
                pltpu.VMEM((nd, rank // nd, rows), f32),
                pltpu.VMEM((nd, rank // nd, rows), f32),
                pltpu.VMEM((nb * cap * rank, rows), bf),
                pltpu.VMEM((chunks, rows, cw), f32),
                dma,
                dma((n * chunks,)),
                dma((2,)),
                dma((2, DEPTH)),
                dma((2, DEPTH)),
                dma((2, steps)),
                dma((2, steps)),
                dma((2, nb - 1)),
                dma((2, nb - 1)),
                dma((4,)),
            ],
            compiler_params=pltpu.CompilerParams(
                collective_id=0, has_side_effects=True, vmem_limit_bytes=56 * 1024 * 1024
            ),
            cost_estimate=pl.CostEstimate(
                flops=2 * rows * depth * w.shape[1], bytes_accessed=2 * w.size, transcendentals=0
            ),
        )(x, w, jnp.swapaxes(down, 1, 2), up, lists, slots.reshape(1, rows))

    in_specs = (
        P(("groups", "batch"), "mp"),
        P("mp", "rep"),
        P("batch", "mp", None),
        P("batch", None, ("rep", "mp")),
        P("groups", None, None),
        P(("groups", "batch")),
    )
    out_specs = P(("groups", "batch"), ("rep", "mp"))
    return jax.shard_map(
        per_device, mesh=mesh, in_specs=in_specs, out_specs=out_specs, check_vma=False
    )
```

```python
import functools

import jax
import jax.numpy as jnp
from jax import lax
from jax.experimental import pallas as pl
from jax.experimental.pallas import tpu as pltpu
from jax.sharding import PartitionSpec as P

MESH = pl.DeviceIdType.MESH
TOP = 32766.0
DEPTH = 2
AHEAD = 2
LAG = 2
OWN = 0


def kernel(
    n, reps, nb, cw,
    x_hbm, w_hbm, a_hbm, b_hbm, lists, slot_ref, out_ref,
    x_v, w_v, a_all, b_all, a_snd, a_tab, b_snd, b_tab,
    snd, snd_scale, rcv, rcv_scale, rs_snd, rs_rcv, ag, spread, acc,
    x_sem, w_sem, ab_sem, snd_sem, snd_scale_sem, rcv_sem, rcv_scale_sem,
    xs_sem, xr_sem, small_sem,
):
    me, rep, mine = lax.axis_index("mp"), lax.axis_index("rep"), lax.axis_index("batch")
    chunks = acc.shape[0]
    steps = (n - 1) * chunks
    cap = lists.shape[2]
    half = cap // reps
    rank = a_tab.shape[2]
    nd = n * reps
    lin = me * reps + rep
    counts = ((n - 1 - me) * chunks, me * chunks)

    def w_copy(q):
        return pltpu.make_async_copy(
            w_hbm.at[:, pl.ds(pl.multiple_of(q * cw, cw), cw)], w_v.at[q], w_sem.at[q]
        )

    def chunk_of(t, d):
        s, c = t // chunks, t % chunks
        return ((n - 1 - s) if d == 0 else s) * chunks + c

    def fetch(tick):
        for d in range(2):
            t = tick - LAG * (me if d == 0 else n - 1 - me)

            @pl.when((t >= 0) & (t < counts[d]))
            def _():
                w_copy(chunk_of(t, d)).start()

    x_copy = pltpu.make_async_copy(x_hbm, x_v, x_sem)
    a_copy = pltpu.make_async_copy(a_hbm, a_all, ab_sem.at[0])
    b_copy = pltpu.make_async_copy(b_hbm, b_all, ab_sem.at[1])
    barrier = pltpu.get_barrier_semaphore()

    x_copy.start()
    for t in range(AHEAD):
        fetch(t)

    def peer(k):
        p = lax.rem(lin + k, nd)
        return p, {"mp": p // reps, "rep": lax.rem(p, reps)}

    for k in range(1, nb):
        pl.semaphore_signal(
            barrier, inc=1, device_id={"batch": lax.rem(mine + k, nb)}, device_id_type=MESH
        )

    def greet(k, carry):
        pl.semaphore_signal(barrier, inc=1, device_id=peer(k)[1], device_id_type=MESH)
        return carry

    lax.fori_loop(1, nd, greet, 0)
    a_copy.start()
    x_copy.wait()

    @pl.when((me == 0) | (me == n - 1))
    def _():
        q = jnp.where(me == 0, (n - 1) * chunks, 0)
        w_copy(q).wait()
        acc[0] = jnp.dot(x_v[...], w_v[q], preferred_element_type=jnp.float32)

    pl.semaphore_wait(barrier, nd - 1 + nb - 1)

    def sends(t, d):
        to = {"mp": me + 1 if d == 0 else me - 1}
        return (
            pltpu.make_async_remote_copy(
                snd.at[d, t % DEPTH], rcv.at[d, t], snd_sem.at[d, t % DEPTH],
                rcv_sem.at[d, t], device_id=to, device_id_type=MESH,
            ),
            pltpu.make_async_remote_copy(
                snd_scale.at[d, t % DEPTH], rcv_scale.at[d, t], snd_scale_sem.at[d, t % DEPTH],
                rcv_scale_sem.at[d, t], device_id=to, device_id_type=MESH,
            ),
        )

    def a_send(k):
        return pltpu.make_async_remote_copy(
            a_snd.at[k - 1], a_tab.at[mine], xs_sem.at[0, k - 1], xr_sem.at[0, k - 1],
            device_id={"batch": lax.rem(mine + k, nb)}, device_id_type=MESH,
        )

    def b_send(k):
        return pltpu.make_async_remote_copy(
            b_snd.at[k - 1], b_tab.at[mine], xs_sem.at[1, k - 1], xr_sem.at[1, k - 1],
            device_id={"batch": lax.rem(mine + k, nb)}, device_id_type=MESH,
        )

    def rs_send(k):
        p, to = peer(k)
        return pltpu.make_async_remote_copy(
            rs_snd.at[p], rs_rcv.at[k - 1], small_sem.at[0], small_sem.at[1],
            device_id=to, device_id_type=MESH,
        )

    def ag_send(k):
        return pltpu.make_async_remote_copy(
            ag.at[lin], ag.at[lin], small_sem.at[2], small_sem.at[3],
            device_id=peer(k)[1], device_id_type=MESH,
        )

    def all_small(buf, i):
        part = buf.at[pl.ds(0, nd - 1)]
        return pltpu.make_async_remote_copy(
            part, part, small_sem.at[i], small_sem.at[i + 1],
            device_id=peer(1)[1], device_id_type=MESH,
        )

    def pick_down():
        a_copy.wait()
        for k in range(1, nb):
            to = lax.rem(mine + k, nb)
            for j in range(half):
                a_snd[k - 1, j] = a_all[lists[to, mine, rep * half + j]]
            a_send(k).start()
        for j in range(half):
            a_tab[mine, j] = a_all[lists[mine, mine, rep * half + j]]

    def pick_up():
        b_copy.wait()
        for k in range(1, nb):
            to = lax.rem(mine + k, nb)
            for j in range(cap):
                b_snd[k - 1, j] = b_all[lists[to, mine, j]]
            b_send(k).start()
        for j in range(cap):
            b_tab[mine, j] = b_all[lists[mine, mine, j]]

    def shrink_part():
        for k in range(1, nb):
            a_send(k).wait()
        total = jnp.zeros((rank, x_v.shape[0]), jnp.float32)
        for h in range(nb):
            every = lax.dot_general(
                a_tab[h].reshape(half * rank, a_tab.shape[3]), x_v[...],
                (((1,), (1,)), ((), ())), preferred_element_type=jnp.float32,
            )
            for j in range(half):
                here = slot_ref[...] == h * cap + rep * half + j
                total += jnp.where(here, every[j * rank:(j + 1) * rank], 0.0)
        rr = rank // nd
        for p in range(nd):
            rs_snd[p] = total[p * rr:(p + 1) * rr]

        def go(k, carry):
            rs_send(k).start()
            return carry

        lax.fori_loop(1, nd, go, 0)

    def shrink_sum():
        all_small(rs_rcv, 0).wait()
        total = rs_snd[lin]
        for k in range(nd - 1):
            total += rs_rcv[k]
        ag[lin] = total.astype(jnp.bfloat16).astype(jnp.float32)

        def go(k, carry):
            ag_send(k).start()
            return carry

        lax.fori_loop(1, nd, go, 0)

    def decoded(d, t):
        for copy in sends(t, d):
            copy.wait_recv()
        return rcv[d, t].astype(jnp.int32).astype(jnp.float32) * rcv_scale[d, t]

    hops = (me, n - 1 - me)

    def step(tick, carry):
        for d in range(2):
            t = tick - LAG * hops[d]

            @pl.when((t + AHEAD >= 0) & (t + AHEAD < counts[d]))
            def _():
                w_copy(chunk_of(t + AHEAD, d)).start()

            @pl.when((t >= 0) & (t < counts[d]))
            def _():
                q = chunk_of(t, d)

                @pl.when(tick > 0)
                def _():
                    w_copy(q).wait()
                    acc[0] = jnp.dot(x_v[...], w_v[q], preferred_element_type=jnp.float32)

                @pl.when(hops[d] > 0)
                def _():
                    acc[0] += decoded(d, t)

                @pl.when(t >= DEPTH)
                def _():
                    for copy in sends(t - DEPTH, d):
                        copy.wait_send()

                value = acc[0]
                most = jnp.maximum(jnp.max(jnp.abs(value), axis=0, keepdims=True), 1e-30)
                code = jnp.round(value * (TOP / most))
                snd[d, t % DEPTH] = code.astype(jnp.int32).astype(jnp.int16)
                snd_scale[d, t % DEPTH] = most * (1.0 / TOP)
                for copy in sends(t, d):
                    copy.start()

        @pl.when(tick == 0)
        def _():
            b_copy.start()

        @pl.when((tick >= OWN) & (tick < OWN + chunks))
        def _():
            w_copy(me * chunks + tick - OWN).start()

        for at, stage in ((1, pick_down), (2, pick_up), (steps // 2, shrink_part), (2 * steps // 3, shrink_sum)):
            pl.when(tick == at)(stage)
        return carry

    lax.fori_loop(0, (n - 1) * max(chunks, LAG) + OWN, step, 0)

    all_small(ag, 2).wait()
    low = ag[...].reshape(rank, x_v.shape[0])
    for s in range(nb * cap):
        here = slot_ref[...] == s
        spread[s * rank:(s + 1) * rank] = jnp.where(here, low, 0.0).astype(jnp.bfloat16)
    for k in range(1, nb):
        b_send(k).wait()
    for c in range(chunks):
        w_copy(me * chunks + c).wait()
        table = b_tab[:, :, :, c * cw:(c + 1) * cw].reshape(nb * cap * rank, cw)
        acc[c] = jnp.dot(
            x_v[...], w_v[me * chunks + c], preferred_element_type=jnp.float32
        ) + 0.5 * lax.dot_general(
            spread[...], table, (((0,), (0,)), ((), ())), preferred_element_type=jnp.float32
        )
    for c in range(chunks):
        for d in range(2):
            @pl.when(me > 0 if d == 0 else me < n - 1)
            def _():
                acc[c] += decoded(d, counts[d] + c)
        out_ref[:, c * cw:(c + 1) * cw] = acc[c].astype(out_ref.dtype)

    for d in range(2):
        def drain(t, carry):
            for copy in sends(t, d):
                copy.wait_send()
            return carry

        lax.fori_loop(jnp.maximum(counts[d] - DEPTH, 0), counts[d], drain, 0)


def solution(mesh):
    n, reps, nb = mesh.shape["mp"], mesh.shape["rep"], mesh.shape["batch"]

    def per_device(x, w, down, up, lists, slots):
        rows, depth = x.shape
        adapters, _, rank = down.shape
        width = up.shape[2]
        cap = lists.shape[2]
        half = cap // reps
        cw = min(256, width)
        chunks = width // cw
        steps = (n - 1) * chunks
        nd = n * reps
        bf, f32 = jnp.bfloat16, jnp.float32
        dma = pltpu.SemaphoreType.DMA
        hbm = pl.BlockSpec(memory_space=pl.ANY)
        vmem = pl.BlockSpec(memory_space=pltpu.VMEM)
        return pl.pallas_call(
            functools.partial(kernel, n, reps, nb, cw),
            out_shape=jax.ShapeDtypeStruct((rows, width), bf),
            in_specs=[hbm] * 4 + [pl.BlockSpec(memory_space=pltpu.SMEM), vmem],
            out_specs=vmem,
            scratch_shapes=[
                pltpu.VMEM((rows, depth), bf),
                pltpu.VMEM((n * chunks, depth, cw), bf),
                pltpu.VMEM((adapters, rank, depth), bf),
                pltpu.VMEM((adapters, rank, width), bf),
                pltpu.VMEM((nb - 1, half, rank, depth), bf),
                pltpu.VMEM((nb, half, rank, depth), bf),
                pltpu.VMEM((nb - 1, cap, rank, width), bf),
                pltpu.VMEM((nb, cap, rank, width), bf),
                pltpu.VMEM((2, DEPTH, rows, cw), jnp.int16),
                pltpu.VMEM((2, DEPTH, 1, cw), f32),
                pltpu.VMEM((2, steps, rows, cw), jnp.int16),
                pltpu.VMEM((2, steps, 1, cw), f32),
                pltpu.VMEM((nd, rank // nd, rows), f32),
                pltpu.VMEM((nd, rank // nd, rows), f32),
                pltpu.VMEM((nd, rank // nd, rows), f32),
                pltpu.VMEM((nb * cap * rank, rows), bf),
                pltpu.VMEM((chunks, rows, cw), f32),
                dma,
                dma((n * chunks,)),
                dma((2,)),
                dma((2, DEPTH)),
                dma((2, DEPTH)),
                dma((2, steps)),
                dma((2, steps)),
                dma((2, nb - 1)),
                dma((2, nb - 1)),
                dma((4,)),
            ],
            compiler_params=pltpu.CompilerParams(
                collective_id=0, has_side_effects=True, vmem_limit_bytes=56 * 1024 * 1024
            ),
            cost_estimate=pl.CostEstimate(
                flops=2 * rows * depth * w.shape[1], bytes_accessed=2 * w.size, transcendentals=0
            ),
        )(x, w, jnp.swapaxes(down, 1, 2), up, lists, slots.reshape(1, rows))

    in_specs = (
        P(("groups", "batch"), "mp"),
        P("mp", "rep"),
        P("batch", "mp", None),
        P("batch", None, ("rep", "mp")),
        P("groups", None, None),
        P(("groups", "batch")),
    )
    out_specs = P(("groups", "batch"), ("rep", "mp"))
    return jax.shard_map(
        per_device, mesh=mesh, in_specs=in_specs, out_specs=out_specs, check_vma=False
    )
```
